32 devices in a mesh: ctx: 16 (over z, y, core), head: 2 (over x).
Axes of the slice: x: 2, y: 2, z: 4, core: 2. Of those that a mesh axis runs over, the one named last changes fastest.
Arguments:
- queries: bfloat16 [10240, 2048], P('ctx', 'head'), may hold values from -8 to 8
- keys: bfloat16 [10240, 2048], P('ctx', 'head'), may hold values from -6 to 6
- values: bfloat16 [10240, 2048], P('ctx', 'head'), may hold values from -6 to 6
- key_weight: bfloat16 [16, 16, 128], P('head'), may hold values from -1.5 to 1.5
- value_weight: bfloat16 [16, 16, 128], P('head'), may hold values from -1.5 to 1.5
Outputs:
- attended: bfloat16 [10240, 2048], P(('ctx', 'head'))
The draws below stay inside these ranges and needn't reach their ends.
All inputs are finite; a program needn't handle non-finite values.
Results may differ from the reference program's by a relative error of at most 0.0061.
Values may be sent and summed in bfloat16 or wider, within the bound.
A program may use at most 128 MiB of HBM per device.

```python
import math
import jax
import jax.numpy as jnp
from jax import lax

HD = 128
HEADS = 16
BLOCK = 640
COMP = 16
PARTNERS = 4
TOKENS = 10240
N_CTX = 16


def draw_queries(key, part):
    blocks = TOKENS // BLOCK
    shape = (blocks, BLOCK, HEADS, HD)
    drawn = 2.2 * jax.random.truncated_normal(jax.random.fold_in(key, 1), -3.6, 3.6, shape, jnp.float32)
    return drawn.reshape(TOKENS, HEADS * HD).astype(jnp.bfloat16)


def draw_keys(key, part):
    blocks = TOKENS // BLOCK
    shape = (blocks, BLOCK, HEADS, HD)
    drawn = jax.random.truncated_normal(jax.random.fold_in(key, 2), -6.0, 6.0, shape, jnp.float32)
    return drawn.reshape(TOKENS, HEADS * HD).astype(jnp.bfloat16)


def level_of(key, dims, cuts, least, largest):
    factor_of, own = 1.0, jax.random.fold_in(key, 6)
    for axis_at, shards_of in cuts:
        draws = jnp.exp(jax.random.uniform(jax.random.fold_in(own, axis_at), (shards_of,), jnp.float32, least / len(cuts), largest / len(cuts)))
        factor_of = factor_of * jnp.repeat(draws, dims[axis_at] // shards_of).reshape([-1 if axis == axis_at else 1 for axis in range(len(dims))])
    return factor_of


def bell_draw(key, shape, width, reach, cuts=(), held_as=jnp.bfloat16):
    loudness = level_of(key, shape, cuts, -0.22, 0.18) if cuts else 1.0
    entries = jax.random.normal(key, shape, jnp.float32) * width * loudness
    return jnp.minimum(jnp.maximum(entries, -reach), reach).astype(held_as)


def setup_inputs(seed: int = 0) -> dict:
    seeds = jax.random.split(jax.random.key(seed), 6)
    return {
        "queries": draw_queries(jax.random.fold_in(seeds[5], 71), 0),
        "keys": draw_keys(jax.random.fold_in(seeds[5], 71), 0),
        "values": bell_draw(seeds[2], (TOKENS, HEADS * HD), 1.0, 6.0, ((0, 16), (1, 2))),
        "key_weight": bell_draw(seeds[3], (HEADS, COMP, HD), COMP ** -0.5, 1.5, ((0, 2),)),
        "value_weight": bell_draw(seeds[4], (HEADS, COMP, HD), COMP ** -0.5, 1.5, ((0, 2),)),
    }


def fold_rows(values_in, weight):
    grouped = values_in.astype(jnp.float32).reshape(TOKENS // COMP, COMP, HEADS, HD)
    folded = jnp.einsum('gjhd,hjd->ghd', grouped, weight.astype(jnp.float32))
    return folded.astype(jnp.bfloat16)

def head_attention(operands):
    query_rows, key_rows, value_rows = operands
    score_scale = 1.0 / math.sqrt(HD)
    scores = jnp.dot(query_rows.astype(jnp.float32), key_rows.astype(jnp.float32).T, preferred_element_type=jnp.float32) * score_scale
    row_top = lax.optimization_barrier(jnp.max(scores, axis=1, keepdims=True))
    weights = jnp.exp(scores - row_top)
    row_total = lax.optimization_barrier(jnp.sum(weights, axis=1, keepdims=True))
    rounded = lax.optimization_barrier(weights.astype(jnp.bfloat16)).astype(jnp.float32)
    mixed_rows = jnp.dot(rounded, value_rows.astype(jnp.float32), preferred_element_type=jnp.float32)
    return mixed_rows / row_total

def reference(queries, keys, values, key_weight, value_weight):
    folded_keys = fold_rows(keys, key_weight)
    folded_values = fold_rows(values, value_weight)
    query_blocks = queries.reshape(N_CTX, BLOCK, HEADS, HD)
    key_blocks = keys.reshape(N_CTX, BLOCK, HEADS, HD)
    value_blocks = values.reshape(N_CTX, BLOCK, HEADS, HD)

    def one_block(block_index):
        chosen = [block_index] + [jnp.bitwise_xor(block_index, jnp.int32(1 << bit_level)) for bit_level in range(PARTNERS)]
        near_keys = jnp.concatenate([key_blocks[picked] for picked in chosen] + [folded_keys], 0)
        near_values = jnp.concatenate([value_blocks[picked] for picked in chosen] + [folded_values], 0)
        operands = (jnp.transpose(query_blocks[block_index], (1, 0, 2)), jnp.transpose(near_keys, (1, 0, 2)), jnp.transpose(near_values, (1, 0, 2)))
        return lax.map(head_attention, operands)
    mixed_all = lax.map(one_block, jnp.arange(N_CTX, dtype=jnp.int32))
    return jnp.transpose(mixed_all, (0, 2, 1, 3)).reshape(TOKENS, HEADS * HD).astype(jnp.bfloat16)
```

```python
import functools
import math

import jax
import jax.numpy as jnp
import numpy as np
from jax import lax
from jax.experimental import pallas as pl
from jax.experimental.pallas import tpu as pltpu
from jax.sharding import PartitionSpec as P

WINDOW = 3


def kernel(dims, q_hbm, k_hbm, v_hbm, kw_ref, vw_ref, bias_ref, out_hbm,
           q_own, kv_own, far, comp, acc, top, stage,
           own_sem, send_sem, recv_sem, comp_send, comp_recv, out_send, out_recv, out_local):
    n_ctx, n_head, heads, rows, width, group, padded = dims
    bits = n_ctx.bit_length() - 1
    groups = rows // group
    part_rows = rows // n_head
    half = rows // 2
    scale = math.log2(math.e) / math.sqrt(width)
    me, side = lax.axis_index("ctx"), lax.axis_index("head")

    def partner(bit):
        step = 1 << bit
        return me + (1 - 2 * ((me // step) % 2)) * step

    def columns(h):
        return pl.ds(pl.multiple_of(h * width, width), width)

    def own_copy(i, h):
        src = (k_hbm, v_hbm, q_hbm)[i].at[:, columns(h)]
        dst = q_own.at[h] if i == 2 else kv_own.at[i, h]
        return pltpu.make_async_copy(src, dst, own_sem.at[i, h])

    def kv_copy(bit, i, h):
        return pltpu.make_async_remote_copy(
            src_ref=(k_hbm, v_hbm)[i].at[:, columns(h)],
            dst_ref=far.at[bit, i, h],
            send_sem=send_sem.at[bit, i, h],
            recv_sem=recv_sem.at[bit, i, h],
            device_id={"ctx": partner(bit)},
            device_id_type=pl.DeviceIdType.MESH,
        )

    def comp_copy(step):
        count = 1 << step
        return pltpu.make_async_remote_copy(
            src_ref=comp.at[pl.ds(0, count)],
            dst_ref=comp.at[pl.ds(count, count)],
            send_sem=comp_send.at[step],
            recv_sem=comp_recv.at[step],
            device_id={"ctx": partner(bits - 1 - step)},
            device_id_type=pl.DeviceIdType.MESH,
        )

    def out_columns(h):
        return pl.ds(pl.multiple_of((side * heads + h) * width, width), width)

    def out_copy(d, h):
        peer = (side + d) % n_head
        return pltpu.make_async_remote_copy(
            src_ref=stage.at[h, pl.ds(pl.multiple_of(peer * part_rows, part_rows), part_rows)],
            dst_ref=out_hbm.at[:, out_columns(h)],
            send_sem=out_send.at[d - 1, h],
            recv_sem=out_recv.at[d - 1, h],
            device_id={"head": peer},
            device_id_type=pl.DeviceIdType.MESH,
        )

    def out_own(h):
        return pltpu.make_async_copy(
            stage.at[h, pl.ds(pl.multiple_of(side * part_rows, part_rows), part_rows)],
            out_hbm.at[:, out_columns(h)],
            out_local.at[h],
        )

    def send_head(h):
        for bit in reversed(range(bits)):
            for i in range(2):
                kv_copy(bit, i, h).start()

    barrier = pltpu.get_barrier_semaphore()
    for bit in range(bits):
        pl.semaphore_signal(barrier, inc=1, device_id={"ctx": partner(bit)},
                            device_id_type=pl.DeviceIdType.MESH)
    for d in range(1, n_head):
        pl.semaphore_signal(barrier, inc=1, device_id={"head": (side + d) % n_head},
                            device_id_type=pl.DeviceIdType.MESH)

    @pl.loop(0, heads)
    def _(h):
        for i in range(3):
            own_copy(i, h).start()

    pl.semaphore_wait(barrier, bits + n_head - 1)
    send_head(0)

    @pl.loop(0, heads)
    def _(h):
        for i, weight in enumerate((kw_ref, vw_ref)):
            own_copy(i, h).wait()
            grouped = kv_own[i, h].astype(jnp.float32).reshape(groups, group, width)
            folded = jnp.sum(grouped * weight[h].astype(jnp.float32)[None], axis=1)
            if padded > groups:
                folded = jnp.concatenate(
                    [folded, jnp.zeros((padded - groups, width), jnp.float32)], 0)
            comp[0, i, h] = folded.astype(jnp.bfloat16)
        own_copy(2, h).wait()

    def attend(h, key_rows, value_rows, bias=None, first=False, last=False):
        ones = jnp.ones((value_rows.shape[0], width), jnp.bfloat16)
        wide = jnp.concatenate([value_rows, ones], 1)
        for t in range(2):
            span = pl.ds(t * half, half)
            scores = lax.dot_general(q_own[h, span], key_rows, (((1,), (1,)), ((), ())),
                                     preferred_element_type=jnp.float32) * scale
            if bias is not None:
                scores = scores + bias
            new_top = jnp.max(scores, axis=1, keepdims=True)
            if not first:
                old_top = top[h, span]
                new_top = jnp.maximum(new_top, old_top)
            weights = jnp.exp2(scores - new_top).astype(jnp.bfloat16)
            summed = jnp.dot(weights, wide, preferred_element_type=jnp.float32)
            if not first:
                summed = summed + acc[h, span] * jnp.exp2(old_top - new_top)
            if last:
                stage[h, span] = (summed[:, :width] / summed[:, width:]).astype(jnp.bfloat16)
            else:
                acc[h, span] = summed
                top[h, span] = new_top

    cuts = [heads * s // bits for s in range(bits + 1)]
    for step in range(bits):
        comp_copy(step).start()
        if step + 1 < min(WINDOW, heads):
            send_head(step + 1)

        @pl.loop(cuts[step], cuts[step + 1])
        def _(h):
            attend(h, kv_own[0, h], kv_own[1, h], first=True)

        comp_copy(step).wait_recv()

    order = list(range(bits))

    @pl.loop(0, heads)
    def _(h):
        flat = n_ctx * padded
        attend(h, comp[:, 0, h].reshape(flat, width), comp[:, 1, h].reshape(flat, width),
               bias=bias_ref[0:1, :])
        for bit in order:
            for i in range(2):
                kv_copy(bit, i, h).wait_recv()
            if bit == order[-1]:
                @pl.when(h + WINDOW < heads)
                def _():
                    send_head(h + WINDOW)
            attend(h, far[bit, 0, h], far[bit, 1, h], last=bit == order[-1])
        for d in range(1, n_head):
            out_copy(d, h).start()
        out_own(h).start()

    for step in range(bits):
        comp_copy(step).wait_send()

    @pl.loop(0, heads)
    def _(h):
        for bit in range(bits):
            for i in range(2):
                kv_copy(bit, i, h).wait_send()
        for d in range(1, n_head):
            out_copy(d, h).wait()
        out_own(h).wait()


def body(n_ctx, n_head, queries, keys, values, key_weight, value_weight):
    rows, channels = queries.shape
    heads, group, width = key_weight.shape
    bits = n_ctx.bit_length() - 1
    groups = rows // group
    padded = -(-groups // 16) * 16
    dims = (n_ctx, n_head, heads, rows, width, group, padded)
    flat = n_ctx * padded
    bias = np.where(np.arange(flat) % padded < groups, 0.0, -np.inf).astype(np.float32)
    bias = jnp.asarray(np.broadcast_to(bias, (8, flat)))
    dma = pltpu.SemaphoreType.DMA
    anywhere = pl.BlockSpec(memory_space=pl.ANY)
    vmem = pl.BlockSpec(memory_space=pltpu.VMEM)
    pairs = rows * heads * (bits + 1) * rows + rows * heads * flat
    return pl.pallas_call(
        functools.partial(kernel, dims),
        out_shape=jax.ShapeDtypeStruct((rows // n_head, channels * n_head), jnp.bfloat16),
        in_specs=[anywhere] * 3 + [vmem] * 3,
        out_specs=anywhere,
        scratch_shapes=[
            pltpu.VMEM((heads, rows, width), jnp.bfloat16),
            pltpu.VMEM((2, heads, rows, width), jnp.bfloat16),
            pltpu.VMEM((bits, 2, heads, rows, width), jnp.bfloat16),
            pltpu.VMEM((n_ctx, 2, heads, padded, width), jnp.bfloat16),
            pltpu.VMEM((heads, rows, 2 * width), jnp.float32),
            pltpu.VMEM((heads, rows, 1), jnp.float32),
            pltpu.VMEM((heads, rows, width), jnp.bfloat16),
            dma((3, heads)),
            dma((bits, 2, heads)),
            dma((bits, 2, heads)),
            dma((bits,)),
            dma((bits,)),
            dma((n_head - 1, heads)),
            dma((n_head - 1, heads)),
            dma((heads,)),
        ],
        compiler_params=pltpu.CompilerParams(
            collective_id=0, has_side_effects=True, vmem_limit_bytes=56 * 1024 * 1024),
        cost_estimate=pl.CostEstimate(
            flops=4 * pairs * width, bytes_accessed=8 * rows * channels, transcendentals=pairs),
    )(queries, keys, values, key_weight, value_weight, bias)


def solution(mesh):
    in_specs = (
        P("ctx", "head"),
        P("ctx", "head"),
        P("ctx", "head"),
        P("head", None, None),
        P("head", None, None),
    )
    out_specs = P(("ctx", "head"), None)
    inner = functools.partial(body, mesh.shape["ctx"], mesh.shape["head"])
    return jax.shard_map(inner, mesh=mesh, in_specs=in_specs, out_specs=out_specs, check_vma=False)
```

```python
import functools
import math

import jax
import jax.numpy as jnp
from jax import lax
from jax.experimental import pallas as pl
from jax.experimental.pallas import tpu as pltpu
from jax.sharding import PartitionSpec as P

FAR_WINDOW = 5
NEAR_WINDOW = 5


def kernel(dims, q_hbm, k_hbm, v_hbm, kw_ref, vw_ref, out_hbm,
           q_own, kv_own, far, comp, acc, top, stage,
           own_sem, send_sem, recv_sem, comp_send, comp_recv, out_send, out_recv, out_local):
    n_ctx, n_head, heads, rows, width, group, padded = dims
    bits = n_ctx.bit_length() - 1
    groups = rows // group
    part_rows = rows // n_head
    half = rows // 2
    scale = math.log2(math.e) / math.sqrt(width)
    me, side = lax.axis_index("ctx"), lax.axis_index("head")

    def partner(bit):
        step = 1 << bit
        return me + (1 - 2 * ((me // step) % 2)) * step

    def columns(h):
        return pl.ds(pl.multiple_of(h * width, width), width)

    def own_copy(i, h):
        src = (k_hbm, v_hbm, q_hbm)[i].at[:, columns(h)]
        dst = q_own.at[h] if i == 2 else kv_own.at[i, h]
        return pltpu.make_async_copy(src, dst, own_sem.at[i, h])

    def kv_copy(bit, i, h):
        return pltpu.make_async_remote_copy(
            src_ref=(k_hbm, v_hbm)[i].at[:, columns(h)],
            dst_ref=far.at[bit, i, h],
            send_sem=send_sem.at[bit, i, h],
            recv_sem=recv_sem.at[bit, i, h],
            device_id={"ctx": partner(bit)},
            device_id_type=pl.DeviceIdType.MESH,
        )

    def comp_copy(step):
        count = 1 << step
        return pltpu.make_async_remote_copy(
            src_ref=comp.at[pl.ds(0, count)],
            dst_ref=comp.at[pl.ds(count, count)],
            send_sem=comp_send.at[step],
            recv_sem=comp_recv.at[step],
            device_id={"ctx": partner(bits - 1 - step)},
            device_id_type=pl.DeviceIdType.MESH,
        )

    def out_columns(h):
        return pl.ds(pl.multiple_of((side * heads + h) * width, width), width)

    def out_copy(d, h):
        peer = (side + d) % n_head
        return pltpu.make_async_remote_copy(
            src_ref=stage.at[h, pl.ds(pl.multiple_of(peer * part_rows, part_rows), part_rows)],
            dst_ref=out_hbm.at[:, out_columns(h)],
            send_sem=out_send.at[d - 1, h],
            recv_sem=out_recv.at[d - 1, h],
            device_id={"head": peer},
            device_id_type=pl.DeviceIdType.MESH,
        )

    def out_own(h):
        return pltpu.make_async_copy(
            stage.at[h, pl.ds(pl.multiple_of(side * part_rows, part_rows), part_rows)],
            out_hbm.at[:, out_columns(h)],
            out_local.at[h],
        )

    windows = [min(heads, NEAR_WINDOW)] * (bits - 1) + [min(heads, FAR_WINDOW)]

    def send_first(h):
        for bit in reversed(range(bits)):
            if h < windows[bit]:
                for i in range(2):
                    kv_copy(bit, i, h).start()

    def send_next(h):
        for bit in reversed(range(bits)):
            @pl.when(h + windows[bit] < heads)
            def _():
                for i in range(2):
                    kv_copy(bit, i, h + windows[bit]).start()

    barrier = pltpu.get_barrier_semaphore()
    for bit in range(bits):
        pl.semaphore_signal(barrier, inc=1, device_id={"ctx": partner(bit)},
                            device_id_type=pl.DeviceIdType.MESH)
    for d in range(1, n_head):
        pl.semaphore_signal(barrier, inc=1, device_id={"head": (side + d) % n_head},
                            device_id_type=pl.DeviceIdType.MESH)

    @pl.loop(0, heads)
    def _(h):
        for i in range(3):
            own_copy(i, h).start()

    pl.semaphore_wait(barrier, bits + n_head - 1)
    send_first(0)

    @pl.loop(0, heads)
    def _(h):
        for i, weight in enumerate((kw_ref, vw_ref)):
            own_copy(i, h).wait()
            grouped = kv_own[i, h].astype(jnp.float32).reshape(groups, group, width)
            folded = jnp.sum(grouped * weight[h].astype(jnp.float32)[None], axis=1)
            if padded > groups:
                folded = jnp.concatenate(
                    [folded, jnp.zeros((padded - groups, width), jnp.float32)], 0)
            comp[0, i, h] = folded.astype(jnp.bfloat16)
        own_copy(2, h).wait()

    def attend(h, key_rows, value_rows, bias=None, first=False, last=False):
        ones = jnp.ones((value_rows.shape[0], width), jnp.bfloat16)
        wide = jnp.concatenate([value_rows, ones], 1)
        for t in range(2):
            span = pl.ds(t * half, half)
            scores = lax.dot_general(q_own[h, span], key_rows, (((1,), (1,)), ((), ())),
                                     preferred_element_type=jnp.float32) * scale
            if bias is not None:
                scores = scores + bias
            new_top = jnp.max(scores, axis=1, keepdims=True)
            if not first:
                old_top = top[h, span]
                new_top = jnp.maximum(new_top, old_top)
            weights = jnp.exp2(scores - new_top).astype(jnp.bfloat16)
            summed = jnp.dot(weights, wide, preferred_element_type=jnp.float32)
            if not first:
                summed = summed + acc[h, span] * jnp.exp2(old_top - new_top)
            if last:
                stage[h, span] = (summed[:, :width] / summed[:, width:]).astype(jnp.bfloat16)
            else:
                acc[h, span] = summed
                top[h, span] = new_top

    cuts = [heads * s // bits for s in range(bits + 1)]
    for step in range(bits):
        comp_copy(step).start()
        for h in range(step + 1, step + 2 if step + 1 < bits else heads):
            send_first(h)

        @pl.loop(cuts[step], cuts[step + 1])
        def _(h):
            attend(h, kv_own[0, h], kv_own[1, h], first=True)

        comp_copy(step).wait_recv()

    order = list(range(bits))

    @pl.loop(0, heads)
    def _(h):
        flat = n_ctx * padded
        place = lax.broadcasted_iota(jnp.int32, (1, flat), 1)
        bias = jnp.where(lax.rem(place, padded) < groups, 0.0, -jnp.inf)
        attend(h, comp[:, 0, h].reshape(flat, width), comp[:, 1, h].reshape(flat, width),
               bias=bias)
        for bit in order:
            for i in range(2):
                kv_copy(bit, i, h).wait_recv()
            if bit == order[-1]:
                send_next(h)
            attend(h, far[bit, 0, h], far[bit, 1, h], last=bit == order[-1])
        for d in range(1, n_head):
            out_copy(d, h).start()
        out_own(h).start()

    for step in range(bits):
        comp_copy(step).wait_send()

    @pl.loop(0, heads)
    def _(h):
        for bit in range(bits):
            for i in range(2):
                kv_copy(bit, i, h).wait_send()
        for d in range(1, n_head):
            out_copy(d, h).wait()
        out_own(h).wait()


def body(n_ctx, n_head, queries, keys, values, key_weight, value_weight):
    rows, channels = queries.shape
    heads, group, width = key_weight.shape
    bits = n_ctx.bit_length() - 1
    groups = rows // group
    padded = -(-groups // 16) * 16
    dims = (n_ctx, n_head, heads, rows, width, group, padded)
    flat = n_ctx * padded
    dma = pltpu.SemaphoreType.DMA
    anywhere = pl.BlockSpec(memory_space=pl.ANY)
    vmem = pl.BlockSpec(memory_space=pltpu.VMEM)
    pairs = rows * heads * (bits + 1) * rows + rows * heads * flat
    return pl.pallas_call(
        functools.partial(kernel, dims),
        out_shape=jax.ShapeDtypeStruct((rows // n_head, channels * n_head), jnp.bfloat16),
        in_specs=[anywhere] * 3 + [vmem] * 2,
        out_specs=anywhere,
        scratch_shapes=[
            pltpu.VMEM((heads, rows, width), jnp.bfloat16),
            pltpu.VMEM((2, heads, rows, width), jnp.bfloat16),
            pltpu.VMEM((bits, 2, heads, rows, width), jnp.bfloat16),
            pltpu.VMEM((n_ctx, 2, heads, padded, width), jnp.bfloat16),
            pltpu.VMEM((heads, rows, 2 * width), jnp.float32),
            pltpu.VMEM((heads, rows, 1), jnp.float32),
            pltpu.VMEM((heads, rows, width), jnp.bfloat16),
            dma((3, heads)),
            dma((bits, 2, heads)),
            dma((bits, 2, heads)),
            dma((bits,)),
            dma((bits,)),
            dma((n_head - 1, heads)),
            dma((n_head - 1, heads)),
            dma((heads,)),
        ],
        compiler_params=pltpu.CompilerParams(
            collective_id=0, has_side_effects=True, vmem_limit_bytes=56 * 1024 * 1024),
        cost_estimate=pl.CostEstimate(
            flops=4 * pairs * width, bytes_accessed=8 * rows * channels, transcendentals=pairs),
    )(queries, keys, values, key_weight, value_weight)


def solution(mesh):
    in_specs = (
        P("ctx", "head"),
        P("ctx", "head"),
        P("ctx", "head"),
        P("head", None, None),
        P("head", None, None),
    )
    out_specs = P(("ctx", "head"), None)
    inner = functools.partial(body, mesh.shape["ctx"], mesh.shape["head"])
    return jax.shard_map(inner, mesh=mesh, in_specs=in_specs, out_specs=out_specs, check_vma=False)
```

```python
import functools
import math

import jax
import jax.numpy as jnp
from jax import lax
from jax.experimental import pallas as pl
from jax.experimental.pallas import tpu as pltpu
from jax.sharding import PartitionSpec as P

FAR_WINDOW = 6
SKEW = 2
NEAR_WINDOW = 5


def kernel(dims, q_hbm, k_hbm, v_hbm, kw_ref, vw_ref, out_hbm,
           q_own, kv_own, far, comp, acc, top, stage,
           own_sem, send_sem, recv_sem, comp_send, comp_recv, out_send, out_recv, out_local):
    n_ctx, n_head, heads, rows, width, group, padded = dims
    bits = n_ctx.bit_length() - 1
    groups = rows // group
    part_rows = rows // n_head
    half = rows // 2
    scale = math.log2(math.e) / math.sqrt(width)
    me, side = lax.axis_index("ctx"), lax.axis_index("head")

    def partner(bit):
        step = 1 << bit
        return me + (1 - 2 * ((me // step) % 2)) * step

    def columns(h):
        return pl.ds(pl.multiple_of(h * width, width), width)

    def own_copy(i, h):
        src = (k_hbm, v_hbm, q_hbm)[i].at[:, columns(h)]
        dst = q_own.at[h] if i == 2 else kv_own.at[i, h]
        return pltpu.make_async_copy(src, dst, own_sem.at[i, h])

    def kv_copy(bit, i, h):
        return pltpu.make_async_remote_copy(
            src_ref=(k_hbm, v_hbm)[i].at[:, columns(h)],
            dst_ref=far.at[bit, i, h],
            send_sem=send_sem.at[bit, i, h],
            recv_sem=recv_sem.at[bit, i, h],
            device_id={"ctx": partner(bit)},
            device_id_type=pl.DeviceIdType.MESH,
        )

    def comp_copy(step):
        count = 1 << step
        return pltpu.make_async_remote_copy(
            src_ref=comp.at[pl.ds(0, count)],
            dst_ref=comp.at[pl.ds(count, count)],
            send_sem=comp_send.at[step],
            recv_sem=comp_recv.at[step],
            device_id={"ctx": partner(bits - 1 - step)},
            device_id_type=pl.DeviceIdType.MESH,
        )

    def out_columns(h):
        return pl.ds(pl.multiple_of((side * heads + h) * width, width), width)

    def out_copy(d, h):
        peer = (side + d) % n_head
        return pltpu.make_async_remote_copy(
            src_ref=stage.at[h, pl.ds(pl.multiple_of(peer * part_rows, part_rows), part_rows)],
            dst_ref=out_hbm.at[:, out_columns(h)],
            send_sem=out_send.at[d - 1, h],
            recv_sem=out_recv.at[d - 1, h],
            device_id={"head": peer},
            device_id_type=pl.DeviceIdType.MESH,
        )

    def out_own(h):
        return pltpu.make_async_copy(
            stage.at[h, pl.ds(pl.multiple_of(side * part_rows, part_rows), part_rows)],
            out_hbm.at[:, out_columns(h)],
            out_local.at[h],
        )

    windows = [min(heads, NEAR_WINDOW)] * (bits - 1) + [min(heads, FAR_WINDOW)]

    def send_first(h):
        for bit in reversed(range(bits)):
            if h < windows[bit]:
                for i in range(2):
                    kv_copy(bit, i, h).start()

    def send_next(h, chosen):
        for bit in reversed(chosen):
            @pl.when(h + windows[bit] < heads)
            def _():
                for i in range(2):
                    kv_copy(bit, i, h + windows[bit]).start()

    barrier = pltpu.get_barrier_semaphore()
    for bit in range(bits):
        pl.semaphore_signal(barrier, inc=1, device_id={"ctx": partner(bit)},
                            device_id_type=pl.DeviceIdType.MESH)
    for d in range(1, n_head):
        pl.semaphore_signal(barrier, inc=1, device_id={"head": (side + d) % n_head},
                            device_id_type=pl.DeviceIdType.MESH)

    @pl.loop(0, heads)
    def _(h):
        for i in range(3):
            own_copy(i, h).start()

    pl.semaphore_wait(barrier, bits + n_head - 1)
    send_first(0)

    @pl.loop(0, heads)
    def _(h):
        for i, weight in enumerate((kw_ref, vw_ref)):
            own_copy(i, h).wait()
            grouped = kv_own[i, h].astype(jnp.float32).reshape(groups, group, width)
            folded = jnp.sum(grouped * weight[h].astype(jnp.float32)[None], axis=1)
            if padded > groups:
                folded = jnp.concatenate(
                    [folded, jnp.zeros((padded - groups, width), jnp.float32)], 0)
            comp[0, i, h] = folded.astype(jnp.bfloat16)
        own_copy(2, h).wait()

    def attend(h, key_rows, value_rows, bias=None, first=False, last=False):
        ones = jnp.ones((value_rows.shape[0], width), jnp.bfloat16)
        wide = jnp.concatenate([value_rows, ones], 1)
        for t in range(2):
            span = pl.ds(t * half, half)
            scores = lax.dot_general(q_own[h, span], key_rows, (((1,), (1,)), ((), ())),
                                     preferred_element_type=jnp.float32) * scale
            if bias is not None:
                scores = scores + bias
            new_top = jnp.max(scores, axis=1, keepdims=True)
            if not first:
                old_top = top[h, span]
                new_top = jnp.maximum(new_top, old_top)
            weights = jnp.exp2(scores - new_top).astype(jnp.bfloat16)
            summed = jnp.dot(weights, wide, preferred_element_type=jnp.float32)
            if not first:
                summed = summed + acc[h, span] * jnp.exp2(old_top - new_top)
            if last:
                stage[h, span] = (summed[:, :width] / summed[:, width:]).astype(jnp.bfloat16)
            else:
                acc[h, span] = summed
                top[h, span] = new_top

    cuts = [heads * s // bits for s in range(bits + 1)]
    for step in range(bits):
        comp_copy(step).start()
        for h in range(step + 1, step + 2 if step + 1 < bits else heads):
            send_first(h)

        @pl.loop(cuts[step], cuts[step + 1])
        def _(h):
            attend(h, kv_own[0, h], kv_own[1, h], first=True)

        comp_copy(step).wait_recv()

    def take(h, chosen):
        for bit in chosen:
            for i in range(2):
                kv_copy(bit, i, h).wait_recv()
            if bit == chosen[-1]:
                send_next(h, chosen)
            attend(h, far[bit, 0, h], far[bit, 1, h], last=bit == bits - 1)

    skew = min(heads, SKEW)

    @pl.loop(0, heads + skew)
    def _(turn):
        @pl.when(turn < heads)
        def _():
            h = turn
            flat = n_ctx * padded
            place = lax.broadcasted_iota(jnp.int32, (1, flat), 1)
            bias = jnp.where(lax.rem(place, padded) < groups, 0.0, -jnp.inf)
            attend(h, comp[:, 0, h].reshape(flat, width), comp[:, 1, h].reshape(flat, width),
                   bias=bias)
            take(h, list(range(bits - 2)))

        @pl.when(turn >= skew)
        def _():
            h = turn - skew
            take(h, [bits - 2, bits - 1])
            for d in range(1, n_head):
                out_copy(d, h).start()
            out_own(h).start()

    for step in range(bits):
        comp_copy(step).wait_send()

    @pl.loop(0, heads)
    def _(h):
        for bit in range(bits):
            for i in range(2):
                kv_copy(bit, i, h).wait_send()
        for d in range(1, n_head):
            out_copy(d, h).wait()
        out_own(h).wait()


def body(n_ctx, n_head, queries, keys, values, key_weight, value_weight):
    rows, channels = queries.shape
    heads, group, width = key_weight.shape
    bits = n_ctx.bit_length() - 1
    groups = rows // group
    padded = -(-groups // 16) * 16
    dims = (n_ctx, n_head, heads, rows, width, group, padded)
    flat = n_ctx * padded
    dma = pltpu.SemaphoreType.DMA
    anywhere = pl.BlockSpec(memory_space=pl.ANY)
    vmem = pl.BlockSpec(memory_space=pltpu.VMEM)
    pairs = rows * heads * (bits + 1) * rows + rows * heads * flat
    return pl.pallas_call(
        functools.partial(kernel, dims),
        out_shape=jax.ShapeDtypeStruct((rows // n_head, channels * n_head), jnp.bfloat16),
        in_specs=[anywhere] * 3 + [vmem] * 2,
        out_specs=anywhere,
        scratch_shapes=[
            pltpu.VMEM((heads, rows, width), jnp.bfloat16),
            pltpu.VMEM((2, heads, rows, width), jnp.bfloat16),
            pltpu.VMEM((bits, 2, heads, rows, width), jnp.bfloat16),
            pltpu.VMEM((n_ctx, 2, heads, padded, width), jnp.bfloat16),
            pltpu.VMEM((heads, rows, 2 * width), jnp.float32),
            pltpu.VMEM((heads, rows, 1), jnp.float32),
            pltpu.VMEM((heads, rows, width), jnp.bfloat16),
            dma((3, heads)),
            dma((bits, 2, heads)),
            dma((bits, 2, heads)),
            dma((bits,)),
            dma((bits,)),
            dma((n_head - 1, heads)),
            dma((n_head - 1, heads)),
            dma((heads,)),
        ],
        compiler_params=pltpu.CompilerParams(
            collective_id=0, has_side_effects=True, vmem_limit_bytes=56 * 1024 * 1024),
        cost_estimate=pl.CostEstimate(
            flops=4 * pairs * width, bytes_accessed=8 * rows * channels, transcendentals=pairs),
    )(queries, keys, values, key_weight, value_weight)


def solution(mesh):
    in_specs = (
        P("ctx", "head"),
        P("ctx", "head"),
        P("ctx", "head"),
        P("head", None, None),
        P("head", None, None),
    )
    out_specs = P(("ctx", "head"), None)
    inner = functools.partial(body, mesh.shape["ctx"], mesh.shape["head"])
    return jax.shard_map(inner, mesh=mesh, in_specs=in_specs, out_specs=out_specs, check_vma=False)
```
